256 devices in a mesh: dp: 4 (over z_lo, core), row: 4 (over z_hi), col: 16 (over y, x).
Axes of the slice: x: 4, y: 4, z: 8 (z_hi: 4, z_lo: 2; z = z_hi * 2 + z_lo), core: 2. Of those that a mesh axis runs over, the one named last changes fastest.
Arguments:
- inputs: bfloat16 [2048, 8192], P(('dp', 'col'), 'row'), may hold values from -6 to 6
- w_in: bfloat16 [8192, 16384], P('row', 'col'), may hold values from -0.0625 to 0.0625
- w_out: bfloat16 [16384, 8192], P('col', 'row'), may hold values from -0.046875 to 0.046875
- grad_outputs: bfloat16 [2048, 8192], P(('dp', 'col'), 'row'), may hold values from -6 to 6
Outputs:
- outputs: bfloat16 [2048, 8192], P(('dp', 'col'), 'row')
- grad_inputs: bfloat16 [2048, 8192], P(('dp', 'col'), 'row')
- grad_w_in: bfloat16 [8192, 16384], P(('row', 'dp'), 'col')
- grad_w_out: bfloat16 [16384, 8192], P('col', ('row', 'dp'))
The draws below stay inside these ranges and needn't reach their ends.
All inputs are finite; a program needn't handle non-finite values.
Results may differ from the reference program's by a relative error of at most 0.024.
Values may be sent and summed in bfloat16 or wider, within the bound.
No kernel may reach another device: no remote copies, remote signals or barrier semaphores. Data moves between devices by JAX's collectives and lax.ppermute only.
A program may use at most 128 MiB of HBM per device.

```python
import jax
import jax.numpy as jnp
from jax import lax

D = 8192
FF = 16384
TOKENS = 2048


def steps_of(key, extent, split, least, largest):
    factor_of = 1.0
    for axis_at, parts in split:
        steps = jax.random.uniform(jax.random.fold_in(jax.random.fold_in(key, 6), axis_at), (parts,), jnp.float32, least / len(split), largest / len(split))
        factor_of = factor_of * jnp.repeat(jnp.exp(steps), extent[axis_at] // parts).reshape((-1,) + (1,) * (len(extent) - 1 - axis_at))
    return factor_of


def noise(rng, extent, deviation, bound, split=(), kind=jnp.bfloat16):
    result = jax.random.normal(rng, extent, jnp.float32) * deviation
    if len(split) > 0:
        result = steps_of(rng, extent, split, -0.22, 0.18) * result
    return jnp.clip(result, min=-bound, max=bound).astype(kind)


def setup_inputs(seed: int = 0) -> dict:
    splits = jax.random.split(jax.random.key(seed), 5)
    return {
        "inputs": noise(splits[0], (TOKENS, D), 1.0, 6.0, ((0, 64), (1, 4))),
        "w_in": noise(splits[1], (D, FF), D ** -0.5, 0.0625, ((0, 4), (1, 16))),
        "w_out": noise(splits[2], (FF, D), FF ** -0.5, 0.046875, ((0, 16), (1, 4))),
        "grad_outputs": noise(splits[3], (TOKENS, D), 1.0, 6.0, ((0, 64), (1, 4))),
    }


def gelu_fn(values):
    return jax.nn.gelu(values, approximate=True)

def contract(left, right, left_dim, right_dim):
    return lax.dot_general(left, right, (((left_dim,), (right_dim,)), ((), ())), preferred_element_type=jnp.float32)

def reference(inputs, w_in, w_out, grad_outputs):
    preact = jnp.dot(inputs, w_in, preferred_element_type=jnp.float32)
    activated = gelu_fn(preact).astype(jnp.bfloat16)
    outputs = (inputs.astype(jnp.float32) + jnp.dot(activated, w_out, preferred_element_type=jnp.float32)).astype(jnp.bfloat16)
    grad_activated = contract(grad_outputs, w_out, 1, 1)
    grad_preact = jax.vjp(gelu_fn, preact)[1](grad_activated)[0].astype(jnp.bfloat16)
    grad_inputs = (grad_outputs.astype(jnp.float32) + contract(grad_preact, w_in, 1, 1)).astype(jnp.bfloat16)
    grad_w_in = contract(inputs, grad_preact, 0, 0).astype(jnp.bfloat16)
    grad_w_out = contract(activated, grad_outputs, 0, 0).astype(jnp.bfloat16)
    return (outputs, grad_inputs, grad_w_in, grad_w_out)
```

```python
import jax
import jax.numpy as jnp
from jax import lax
from jax.sharding import Mesh, PartitionSpec as P

F32 = jnp.float32
BF16 = jnp.bfloat16
NAMES = ("zl", "core", "zh", "y", "x")
Z = ("zh", "zl")


def gelu_fn(values):
    return jax.nn.gelu(values, approximate=True)


def contract(left, right, left_dim, right_dim):
    return lax.dot_general(
        left, right, (((left_dim,), (right_dim,)), ((), ())), preferred_element_type=F32
    )


def shift(value, axis, step, size):
    return lax.ppermute(value, axis, [(i, (i + step) % size) for i in range(size)])


def gather4(own, axis):
    half = own.shape[0] // 2
    after = shift(own, axis, -1, 4)
    before = shift(own, axis, 1, 4)
    far_low = shift(after[:half], axis, -1, 4)
    far_high = shift(before[half:], axis, 1, 4)
    return [own, after, far_low, far_high, before]


def scatter4(value, axis):
    rows = value.shape[0] // 4
    half = rows // 2
    mine, after, far, before = (value[k * rows : (k + 1) * rows] for k in range(4))
    from_before = shift(far[:half], axis, 1, 4)
    from_after = shift(far[half:], axis, -1, 4)
    add = lambda a, b: (a.astype(F32) + b.astype(F32)).astype(BF16)
    to_after = jnp.concatenate([add(after[:half], from_before), after[half:]])
    to_before = jnp.concatenate([before[:half], add(before[half:], from_after)])
    got_before = shift(to_after, axis, 1, 4)
    got_after = shift(to_before, axis, -1, 4)
    return mine.astype(F32) + (got_before.astype(F32) + got_after.astype(F32))


def to_width(own, zl):
    half = own.shape[1] // 2
    kept = lax.dynamic_slice_in_dim(own, zl * half, half, 1)
    sent = lax.dynamic_slice_in_dim(own, (1 - zl) * half, half, 1)
    got = shift(sent, "zl", 1, 2)
    return jnp.where(zl == 0, kept, got), jnp.where(zl == 0, got, kept)


def to_tokens(first, second, zl):
    kept = jnp.where(zl == 0, first, second)
    sent = jnp.where(zl == 0, second, first).astype(BF16)
    got = shift(sent, "zl", 1, 2).astype(F32)
    return jnp.concatenate(
        [jnp.where(zl == 0, kept, got), jnp.where(zl == 0, got, kept)], axis=1
    )


def gather_plane(first, second):
    xs = jnp.concatenate(gather4(first, "x"))
    ys = jnp.concatenate(gather4(second, "y"))
    return jnp.concatenate(gather4(xs, "y") + gather4(ys, "x"))


def scatter_plane(value):
    rows = value.shape[0] // 2
    ys = scatter4(value[:rows], "y").astype(BF16)
    xs = scatter4(value[rows:], "x").astype(BF16)
    return scatter4(ys, "x"), scatter4(xs, "y")


def shards(inputs, w_in, w_out, grad_outputs):
    zl = lax.axis_index("zl")
    core = lax.axis_index("core")
    half = inputs.shape[1] // 2
    w_in = lax.dynamic_slice_in_dim(w_in, zl * half, half, 0)
    w_out = lax.dynamic_slice_in_dim(w_out, zl * half, half, 1)

    def scatter_z(value):
        return lax.psum_scatter(value.astype(BF16), Z, scatter_dimension=0, tiled=True).astype(F32)

    def gather_z(value):
        return lax.all_gather(value, Z, axis=0, tiled=True)

    tokens = gather_plane(*to_width(inputs, zl))
    preact = scatter_z(contract(tokens, w_in, 1, 0))
    cots = gather_plane(*to_width(grad_outputs, zl))
    grad_activated = scatter_z(contract(cots, w_out, 1, 1))
    activated, back = jax.vjp(gelu_fn, preact)
    all_act = gather_z(activated.astype(BF16))
    out = to_tokens(*scatter_plane(contract(all_act, w_out, 1, 0).astype(BF16)), zl)
    outputs = (inputs.astype(F32) + out).astype(BF16)

    all_grad = gather_z(back(grad_activated)[0].astype(BF16))
    grad = to_tokens(*scatter_plane(contract(all_grad, w_in, 1, 1).astype(BF16)), zl)
    grad_inputs = (grad_outputs.astype(F32) + grad).astype(BF16)

    quarter = half // 2

    def part(value, at):
        return lax.dynamic_slice_in_dim(value, at * quarter, quarter, 1)

    sent = contract(all_act, part(cots, 1 - core), 0, 0).astype(BF16)
    grad_w_out = contract(all_act, part(cots, core), 0, 0) + shift(sent, "core", 1, 2)
    sent = contract(part(tokens, 1 - core), all_grad, 0, 0).astype(BF16)
    grad_w_in = contract(part(tokens, core), all_grad, 0, 0) + shift(sent, "core", 1, 2)
    return (outputs, grad_inputs, grad_w_in.astype(BF16), grad_w_out.astype(BF16))


def solution(mesh):
    fine = Mesh(mesh.devices.reshape(2, 2, 4, 4, 4), NAMES)
    activations = P(("zl", "core", "y", "x"), "zh")
    return jax.shard_map(
        shards,
        mesh=fine,
        in_specs=(activations, P("zh", ("y", "x")), P(("y", "x"), "zh"), activations),
        out_specs=(
            activations,
            activations,
            P(("zh", "zl", "core"), ("y", "x")),
            P(("y", "x"), ("zh", "zl", "core")),
        ),
        check_vma=False,
    )
```

```python
import jax
import jax.numpy as jnp
from jax import lax
from jax.sharding import Mesh, PartitionSpec as P

F32 = jnp.float32
BF16 = jnp.bfloat16
NAMES = ("zl", "core", "zh", "y", "x")
Z = ("zh", "zl")
PLANE = ("core", "y", "x")


def gelu_fn(values):
    return jax.nn.gelu(values, approximate=True)


def contract(left, right, left_dim, right_dim):
    return lax.dot_general(
        left, right, (((left_dim,), (right_dim,)), ((), ())), preferred_element_type=F32
    )


def swap(value, axis):
    return lax.ppermute(value, axis, [(0, 1), (1, 0)])


def shift_z(value, step):
    place = lambda z: (z % 2) * 4 + z // 2
    pairs = [(place(z), place((z + step) % 8)) for z in range(8)]
    return lax.ppermute(value, ("zl", "zh"), pairs)


def shift_plane(value, phase, step):
    pairs = []
    for core in range(2):
        for y in range(4):
            for x in range(4):
                along_x = core == phase
                to_y = y if along_x else (y + step) % 4
                to_x = (x + step) % 4 if along_x else x
                pairs.append((core * 16 + y * 4 + x, core * 16 + to_y * 4 + to_x))
    return lax.ppermute(value, PLANE, pairs)


def add(one, other):
    return (one.astype(F32) + other.astype(F32)).astype(BF16)


def gather4(own, phase):
    return jnp.concatenate([own] + [shift_plane(own, phase, -k) for k in (1, 2, 3)])


def scatter4(value, phase, kept=None):
    rows = value.shape[0] // 4
    blocks = [value[k * rows : (k + 1) * rows] for k in range(4)]
    got = [shift_plane(blocks[k], phase, k).astype(F32) for k in (1, 2, 3)]
    own = blocks[0] if kept is None else kept[:rows]
    return own.astype(F32) + (got[0] + got[1] + got[2])


def gather_plane(own):
    return gather4(gather4(own, 0), 1)


def scatter_ring(value, z, tie=None):
    rows = value.shape[0] // 8
    half = rows // 2

    def block(step, start=0, count=rows):
        return lax.dynamic_slice_in_dim(value, lax.rem(z + 8 + step, 8) * rows + start, count, 0)

    up = shift_z(block(4, 0, half), 1)
    down = shift_z(block(4, half, half), -1)
    up = jnp.concatenate([add(block(3, 0, half), up), block(3, half, half)])
    down = jnp.concatenate([block(-3, 0, half), add(block(-3, half, half), down)])
    up, down = shift_z(up, 1), shift_z(down, -1)
    if tie is not None:
        up, down, tie = lax.optimization_barrier((up, down, tie))
    up, down = shift_z(add(block(2), up), 1), shift_z(add(block(-2), down), -1)
    up, down = shift_z(add(block(1), up), 1), shift_z(add(block(-1), down), -1)
    return block(0).astype(F32) + (up.astype(F32) + down.astype(F32)), tie


def gather_ring(own, z, tie=None):
    rows = own.shape[0]
    half = rows // 2
    out = jnp.zeros((8 * rows, own.shape[1]), own.dtype)

    def put(out, value, step, start=0):
        return lax.dynamic_update_slice_in_dim(
            out, value, lax.rem(z + 8 + step, 8) * rows + start, 0
        )

    out = put(out, own, 0)
    up = down = own
    for step in (1, 2, 3):
        if step == 3 and tie is not None:
            up, down, tie = lax.optimization_barrier((up, down, tie))
        up, down = shift_z(up, 1), shift_z(down, -1)
        out = put(put(out, up, -step), down, step)
    out = put(out, shift_z(up[:half], 1), 4)
    return put(out, shift_z(down[half:], -1), 4, half), tie


def to_width(own, zl):
    half = own.shape[1] // 2
    kept = lax.dynamic_slice_in_dim(own, zl * half, half, 1)
    got = swap(lax.dynamic_slice_in_dim(own, (1 - zl) * half, half, 1), "zl")
    return jnp.concatenate([jnp.where(zl == 0, kept, got), jnp.where(zl == 0, got, kept)])


def to_tokens(value, zl):
    rows = value.shape[0] // 2
    first, second = value[:rows], value[rows:]
    kept = jnp.where(zl == 0, first, second)
    got = swap(jnp.where(zl == 0, second, first).astype(BF16), "zl").astype(F32)
    return jnp.concatenate(
        [jnp.where(zl == 0, kept, got), jnp.where(zl == 0, got, kept)], axis=1
    )


def shards(inputs, w_in, w_out, grad_outputs):
    zl = lax.axis_index("zl")
    core = lax.axis_index("core")
    z = lax.axis_index("zh") * 2 + zl
    half = inputs.shape[1] // 2
    quarter = half // 2
    w_in = lax.dynamic_slice_in_dim(w_in, zl * half, half, 0)
    w_out = lax.dynamic_slice_in_dim(w_out, zl * half, half, 1)

    barrier = lax.optimization_barrier
    tokens = gather_plane(to_width(inputs, zl))
    cot_line = gather4(to_width(grad_outputs, zl), 0)
    tokens, cot_line = barrier((tokens, cot_line))
    part = contract(tokens, w_in, 1, 0).astype(BF16)
    preact, _ = scatter_ring(part, z)
    activated = gelu_fn(preact).astype(BF16)
    preact, activated = barrier((preact, activated))

    cots = gather4(cot_line, 1)
    grad_activated, activated = scatter_ring(
        contract(cots, w_out, 1, 1).astype(BF16), z, activated
    )
    grad_preact = jax.vjp(gelu_fn, preact)[1](grad_activated)[0].astype(BF16)
    all_act, _ = gather_ring(activated, z)
    all_grad, all_act = gather_ring(grad_preact, z, all_act)

    out_line = scatter4(contract(all_act, w_out, 1, 0).astype(BF16), 1).astype(BF16)
    grad_part = contract(all_grad, w_in, 1, 1).astype(BF16)
    out_line, grad_tied = barrier((out_line, grad_part))
    out = to_tokens(scatter4(out_line, 0), zl)
    outputs = (inputs.astype(F32) + out).astype(BF16)
    grad_line = scatter4(grad_part, 1, grad_tied).astype(BF16)
    grad = to_tokens(scatter4(grad_line, 0), zl)
    grad_inputs = (grad_outputs.astype(F32) + grad).astype(BF16)

    def columns(value, at):
        return lax.dynamic_slice_in_dim(value, at * quarter, quarter, 1)

    sent = contract(all_act, columns(cots, 1 - core), 0, 0).astype(BF16)
    grad_w_out = contract(all_act, columns(cots, core), 0, 0) + swap(sent, "core")
    sent = contract(columns(tokens, 1 - core), all_grad, 0, 0).astype(BF16)
    grad_w_in = contract(columns(tokens, core), all_grad, 0, 0) + swap(sent, "core")
    return (outputs, grad_inputs, grad_w_in.astype(BF16), grad_w_out.astype(BF16))


def solution(mesh):
    fine = Mesh(mesh.devices.reshape(2, 2, 4, 4, 4), NAMES)
    activations = P(("zl", "core", "y", "x"), "zh")
    return jax.shard_map(
        shards,
        mesh=fine,
        in_specs=(activations, P("zh", ("y", "x")), P(("y", "x"), "zh"), activations),
        out_specs=(
            activations,
            activations,
            P(("zh", "zl", "core"), ("y", "x")),
            P(("y", "x"), ("zh", "zl", "core")),
        ),
        check_vma=False,
    )
```

```python
import jax
import jax.numpy as jnp
from jax import lax
from jax.sharding import Mesh, PartitionSpec as P

F32 = jnp.float32
BF16 = jnp.bfloat16
NAMES = ("zl", "core", "zh", "y", "x")
barrier = lax.optimization_barrier


def gelu_fn(values):
    return jax.nn.gelu(values, approximate=True)


def contract(left, right, left_dim, right_dim):
    return lax.dot_general(
        left, right, (((left_dim,), (right_dim,)), ((), ())), preferred_element_type=F32
    )


def add(one, other):
    return (one.astype(F32) + other.astype(F32)).astype(BF16)


def swap(value, axis):
    return lax.ppermute(value, axis, [(0, 1), (1, 0)])


def shift_z(value, way):
    place = lambda z, core: (z % 2) * 8 + core * 4 + (z % 8) // 2
    pairs = [
        (place(z, core), place((z + way * (1 - 2 * core)) % 8, core))
        for core in range(2)
        for z in range(8)
    ]
    return lax.ppermute(value, ("zl", "core", "zh"), pairs)


def shift_plane(value, phase, step):
    pairs = []
    for core in range(2):
        for y in range(4):
            for x in range(4):
                along_x = core == phase
                to_y = y if along_x else (y + step) % 4
                to_x = (x + step) % 4 if along_x else x
                pairs.append((core * 16 + y * 4 + x, core * 16 + to_y * 4 + to_x))
    return lax.ppermute(value, ("core", "y", "x"), pairs)


def gather4(own, phase):
    return [own] + [shift_plane(own, phase, -k) for k in (1, 2, 3)]


def scatter4(blocks, phase):
    got = [shift_plane(blocks[k], phase, k).astype(F32) for k in (1, 2, 3)]
    return blocks[0].astype(F32) + (got[0] + got[1] + got[2])


def split4(value):
    rows = value.shape[0] // 4
    return [value[k * rows : (k + 1) * rows] for k in range(4)]


def scatter_ring(value, z, way, ties=()):
    rows = value.shape[0] // 8
    ties = dict(ties)

    def cut(step):
        at = lax.rem(z + 16 + way * step, 8) * rows
        return lax.dynamic_slice_in_dim(value, at, rows, 0)

    steps = (4, 3, -3, 2, -2, 1, -1, 0)
    block = dict(zip(steps, barrier(tuple(cut(step) for step in steps)))).__getitem__

    one = shift_z(block(4), 1)
    other = None
    for step in (3, 2, 1):
        if step in ties:
            if other is None:
                one, ties[step] = barrier((one, ties[step]))
            else:
                one, other, ties[step] = barrier((one, other, ties[step]))
        one = shift_z(add(block(step), one), 1)
        other = shift_z(block(-step) if other is None else add(block(-step), other), -1)
    return (block(0), one, other), ties


def total3(pieces):
    own, one, other = (piece.astype(F32) for piece in pieces)
    return own + (one + other)


def gather_ring(own, z, way, meet=None):
    rows = own.shape[0]
    out = jnp.zeros((8 * rows, own.shape[1]), own.dtype)

    def put(out, value, step):
        at = lax.rem(z + 16 + way * step, 8) * rows
        return lax.dynamic_update_slice_in_dim(out, value, at, 0)

    out = put(out, own, 0)
    one = other = own
    for step in (1, 2, 3):
        one, other = shift_z(one, 1), shift_z(other, -1)
        if step == 1 and meet is not None:
            one, other, meet = barrier((one, other, meet))
        out = put(put(out, one, -step), other, step)
    return put(out, shift_z(one, 1), 4), meet


def shards(inputs, w_in, w_out, grad_outputs):
    zl = lax.axis_index("zl")
    core = lax.axis_index("core")
    z = lax.axis_index("zh") * 2 + zl
    way = 1 - 2 * core
    rows = inputs.shape[0]
    half = inputs.shape[1] // 2
    quarter = half // 2
    low = zl == 0
    w_in = lax.dynamic_slice_in_dim(w_in, zl * half, half, 0)
    w_out = lax.dynamic_slice_in_dim(w_out, zl * half, half, 1)

    with jax.named_scope("width_swap"):
        both = jnp.concatenate([inputs, grad_outputs])
        kept = jnp.where(low, both[:, :half], both[:, half:])
        got = swap(jnp.where(low, both[:, half:], both[:, :half]), "zl")
        first, second = jnp.where(low, kept, got), jnp.where(low, got, kept)
        own = jnp.concatenate([first[:rows], second[:rows], first[rows:], second[rows:]])
    with jax.named_scope("gather_line"):
        line = gather4(own, 0)
    with jax.named_scope("gather_tokens"):
        tokens = jnp.concatenate(gather4(jnp.concatenate([b[: 2 * rows] for b in line]), 1))
    with jax.named_scope("gather_cots"):
        cots = jnp.concatenate(gather4(jnp.concatenate([b[2 * rows :] for b in line]), 1))

    part = contract(tokens, w_in, 1, 0).astype(BF16)
    grad_part = contract(cots, w_out, 1, 1).astype(BF16)
    with jax.named_scope("scatter_preact"):
        pieces, tied = scatter_ring(part, z, way, {3: grad_part})
    grad_part = tied[3]
    preact = total3(pieces)
    activated = gelu_fn(preact).astype(BF16)
    preact, activated = barrier((preact, activated))
    with jax.named_scope("scatter_grad"):
        pieces, tied = scatter_ring(grad_part, z, way, {1: activated})
    activated = tied[1]
    with jax.named_scope("gather_act"):
        all_act, _ = gather_ring(activated, z, way)
    grad_preact = jax.vjp(gelu_fn, preact)[1](total3(pieces))[0].astype(BF16)
    with jax.named_scope("gather_grad"):
        all_grad, _ = gather_ring(grad_preact, z, way)

    out_part = split4(contract(all_act, w_out, 1, 0).astype(BF16))
    grad_part = contract(all_grad, w_in, 1, 1).astype(BF16)
    with jax.named_scope("scatter_out"):
        out_line = scatter4(out_part, 1).astype(BF16)
    with jax.named_scope("scatter_cot"):
        grad_line = scatter4(split4(grad_part), 1).astype(BF16)
    all_act, all_grad, out_line = barrier((all_act, all_grad, out_line))

    def columns(value, at):
        return lax.dynamic_slice_in_dim(value, at * quarter, quarter, 1)

    with jax.named_scope("weight_gradients"):
        sent_out = contract(all_act, columns(cots, 1 - core), 0, 0).astype(BF16)
        sent_in = contract(columns(tokens, 1 - core), all_grad, 0, 0).astype(BF16)
        got_out, got_in = swap(sent_out, "core"), swap(sent_in, "core")
        grad_w_out = (contract(all_act, columns(cots, core), 0, 0) + got_out).astype(BF16)
        grad_w_in = (contract(columns(tokens, core), all_grad, 0, 0) + got_in).astype(BF16)

    lines = [jnp.concatenate([a, b]) for a, b in zip(split4(out_line), split4(grad_line))]
    lines, grad_w_in, grad_w_out = barrier((lines, grad_w_in, grad_w_out))
    with jax.named_scope("scatter_line"):
        total = scatter4(lines, 0)
    with jax.named_scope("token_swap"):
        first = jnp.concatenate([total[:rows], total[2 * rows : 3 * rows]])
        second = jnp.concatenate([total[rows : 2 * rows], total[3 * rows :]])
        kept = jnp.where(low, first, second)
        got = swap(jnp.where(low, second, first).astype(BF16), "zl").astype(F32)
        sums = jnp.concatenate([jnp.where(low, kept, got), jnp.where(low, got, kept)], axis=1)
    outputs = (inputs.astype(F32) + sums[:rows]).astype(BF16)
    grad_inputs = (grad_outputs.astype(F32) + sums[rows:]).astype(BF16)
    return (outputs, grad_inputs, grad_w_in, grad_w_out)


def solution(mesh):
    fine = Mesh(mesh.devices.reshape(2, 2, 4, 4, 4), NAMES)
    activations = P(("zl", "core", "y", "x"), "zh")
    return jax.shard_map(
        shards,
        mesh=fine,
        in_specs=(activations, P("zh", ("y", "x")), P(("y", "x"), "zh"), activations),
        out_specs=(
            activations,
            activations,
            P(("zh", "zl", "core"), ("y", "x")),
            P(("y", "x"), ("zh", "zl", "core")),
        ),
        check_vma=False,
    )
```

```python
import jax
import jax.numpy as jnp
from jax import lax
from jax.sharding import Mesh, PartitionSpec as P

F32 = jnp.float32
BF16 = jnp.bfloat16
NAMES = ("zl", "core", "zh", "y", "x")
barrier = lax.optimization_barrier


def gelu_fn(values):
    return jax.nn.gelu(values, approximate=True)


def contract(left, right, left_dim, right_dim):
    return lax.dot_general(
        left, right, (((left_dim,), (right_dim,)), ((), ())), preferred_element_type=F32
    )


def add(one, other):
    return (one.astype(F32) + other.astype(F32)).astype(BF16)


def swap(value, axis):
    return lax.ppermute(value, axis, [(0, 1), (1, 0)])


def shift_z(value, way):
    place = lambda z, core: (z % 2) * 8 + core * 4 + (z % 8) // 2
    pairs = [
        (place(z, core), place((z + way * (1 - 2 * core)) % 8, core))
        for core in range(2)
        for z in range(8)
    ]
    return lax.ppermute(value, ("zl", "core", "zh"), pairs)


def shift_plane(value, phase, step):
    pairs = []
    for core in range(2):
        for y in range(4):
            for x in range(4):
                along_x = core == phase
                to_y = y if along_x else (y + step) % 4
                to_x = (x + step) % 4 if along_x else x
                pairs.append((core * 16 + y * 4 + x, core * 16 + to_y * 4 + to_x))
    return lax.ppermute(value, ("core", "y", "x"), pairs)


def gather4(own, phase):
    return [own] + [shift_plane(own, phase, -k) for k in (1, 2, 3)]


def scatter4(blocks, phase):
    got = [shift_plane(blocks[k], phase, k).astype(F32) for k in (1, 2, 3)]
    return blocks[0].astype(F32) + (got[0] + got[1] + got[2])


def split4(value):
    rows = value.shape[0] // 4
    return [value[k * rows : (k + 1) * rows] for k in range(4)]


def scatter_ring(value, z, way, ties=()):
    rows = value.shape[0] // 8
    ties = dict(ties)

    def cut(step):
        at = lax.rem(z + 16 + way * step, 8) * rows
        return lax.dynamic_slice_in_dim(value, at, rows, 0)

    steps = (4, 3, -3, 2, -2, 1, -1, 0)
    block = dict(zip(steps, barrier(tuple(cut(step) for step in steps)))).__getitem__

    one, other = shift_z(block(4), 1), None
    for step in (3, 2, 1):
        if step in ties:
            if other is None:
                one, ties[step] = barrier((one, ties[step]))
            else:
                one, other, ties[step] = barrier((one, other, ties[step]))
        one = shift_z(add(block(step), one), 1)
        other = shift_z(block(-step) if other is None else add(block(-step), other), -1)
    return (block(0), one, other), ties


def total3(pieces):
    own, one, other = (piece.astype(F32) for piece in pieces)
    return own + (one + other)


def gather_ring(own, z, way):
    rows = own.shape[0]
    out = jnp.zeros((8 * rows, own.shape[1]), own.dtype)

    def put(out, value, step):
        at = lax.rem(z + 16 + way * step, 8) * rows
        return lax.dynamic_update_slice_in_dim(out, value, at, 0)

    out = put(out, own, 0)
    one = other = own
    for step in (1, 2, 3):
        one, other = shift_z(one, 1), shift_z(other, -1)
        out = put(put(out, one, -step), other, step)
    return put(out, shift_z(one, 1), 4)


def shards(inputs, w_in, w_out, grad_outputs):
    zl = lax.axis_index("zl")
    core = lax.axis_index("core")
    z = lax.axis_index("zh") * 2 + zl
    way = 1 - 2 * core
    rows = inputs.shape[0]
    half = inputs.shape[1] // 2
    quarter = half // 2
    low = zl == 0
    w_in = lax.dynamic_slice_in_dim(w_in, zl * half, half, 0)
    w_out = lax.dynamic_slice_in_dim(w_out, zl * half, half, 1)

    with jax.named_scope("width_swap"):
        both = jnp.concatenate([inputs, grad_outputs])
        kept = jnp.where(low, both[:, :half], both[:, half:])
        got = swap(jnp.where(low, both[:, half:], both[:, :half]), "zl")
        first, second = jnp.where(low, kept, got), jnp.where(low, got, kept)
        own = jnp.concatenate([first[:rows], second[:rows], first[rows:], second[rows:]])
    with jax.named_scope("gather_line"):
        line = gather4(own, 0)
    with jax.named_scope("gather_tokens"):
        tokens = jnp.concatenate(gather4(jnp.concatenate([b[: 2 * rows] for b in line]), 1))
    with jax.named_scope("gather_cots"):
        cots = jnp.concatenate(gather4(jnp.concatenate([b[2 * rows :] for b in line]), 1))

    part = contract(tokens, w_in, 1, 0).astype(BF16)
    grad_part = contract(cots, w_out, 1, 1).astype(BF16)
    with jax.named_scope("scatter_preact"):
        pieces, tied = scatter_ring(part, z, way, {3: grad_part})
    grad_part = tied[3]
    preact = total3(pieces)
    activated = gelu_fn(preact).astype(BF16)
    preact, activated = barrier((preact, activated))
    with jax.named_scope("scatter_grad"):
        pieces, tied = scatter_ring(grad_part, z, way, {1: activated})
    activated = tied[1]
    with jax.named_scope("gather_act"):
        all_act = gather_ring(activated, z, way)
    grad_preact = jax.vjp(gelu_fn, preact)[1](total3(pieces))[0].astype(BF16)
    with jax.named_scope("gather_grad"):
        all_grad = gather_ring(grad_preact, z, way)

    out_part = split4(contract(all_act, w_out, 1, 0).astype(BF16))
    grad_part = contract(all_grad, w_in, 1, 1).astype(BF16)
    with jax.named_scope("scatter_out"):
        out_line = scatter4(out_part, 1).astype(BF16)
    with jax.named_scope("scatter_cot"):
        grad_line = scatter4(split4(grad_part), 1).astype(BF16)
    all_act, all_grad, out_line = barrier((all_act, all_grad, out_line))

    def columns(value, at):
        return lax.dynamic_slice_in_dim(value, at * quarter, quarter, 1)

    with jax.named_scope("weight_gradients"):
        sent_out = contract(all_act, columns(cots, 1 - core), 0, 0).astype(BF16)
        sent_in = contract(columns(tokens, 1 - core), all_grad, 0, 0).astype(BF16)
        got_out, got_in = swap(sent_out, "core"), swap(sent_in, "core")
        grad_w_out = (contract(all_act, columns(cots, core), 0, 0) + got_out).astype(BF16)
        grad_w_in = (contract(columns(tokens, core), all_grad, 0, 0) + got_in).astype(BF16)

    lines = [jnp.concatenate([a, b]) for a, b in zip(split4(out_line), split4(grad_line))]
    with jax.named_scope("scatter_line"):
        got = [shift_plane(lines[k], 0, k) for k in (1, 2, 3)]
        got, grad_w_in, grad_w_out = barrier((got, grad_w_in, grad_w_out))
        got = [value.astype(F32) for value in got]
        total = lines[0].astype(F32) + (got[0] + got[1] + got[2])
    with jax.named_scope("token_swap"):
        first = jnp.concatenate([total[:rows], total[2 * rows : 3 * rows]])
        second = jnp.concatenate([total[rows : 2 * rows], total[3 * rows :]])
        kept = jnp.where(low, first, second)
        got = swap(jnp.where(low, second, first).astype(BF16), "zl").astype(F32)
        sums = jnp.concatenate([jnp.where(low, kept, got), jnp.where(low, got, kept)], axis=1)
    outputs = (inputs.astype(F32) + sums[:rows]).astype(BF16)
    grad_inputs = (grad_outputs.astype(F32) + sums[rows:]).astype(BF16)
    return (outputs, grad_inputs, grad_w_in, grad_w_out)


def solution(mesh):
    fine = Mesh(mesh.devices.reshape(2, 2, 4, 4, 4), NAMES)
    activations = P(("zl", "core", "y", "x"), "zh")
    return jax.shard_map(
        shards,
        mesh=fine,
        in_specs=(activations, P("zh", ("y", "x")), P(("y", "x"), "zh"), activations),
        out_specs=(
            activations,
            activations,
            P(("zh", "zl", "core"), ("y", "x")),
            P(("y", "x"), ("zh", "zl", "core")),
        ),
        check_vma=False,
    )
```

```python
import jax
import jax.numpy as jnp
from jax import lax
from jax.sharding import Mesh, PartitionSpec as P

F32 = jnp.float32
BF16 = jnp.bfloat16
NAMES = ("zl", "core", "zh", "y", "x")
barrier = lax.optimization_barrier


def gelu_fn(values):
    return jax.nn.gelu(values, approximate=True)


def contract(left, right, left_dim, right_dim):
    return lax.dot_general(
        left, right, (((left_dim,), (right_dim,)), ((), ())), preferred_element_type=F32
    )


def add(one, other):
    return (one.astype(F32) + other.astype(F32)).astype(BF16)


def swap(value, axis):
    return lax.ppermute(value, axis, [(0, 1), (1, 0)])


def shift_z(value, way):
    place = lambda z, core: (z % 2) * 8 + core * 4 + (z % 8) // 2
    pairs = [
        (place(z, core), place((z + way * (1 - 2 * core)) % 8, core))
        for core in range(2)
        for z in range(8)
    ]
    return lax.ppermute(value, ("zl", "core", "zh"), pairs)


def shift_plane(value, phase, step):
    pairs = []
    for core in range(2):
        for y in range(4):
            for x in range(4):
                along_x = core == phase
                to_y = y if along_x else (y + step) % 4
                to_x = (x + step) % 4 if along_x else x
                pairs.append((core * 16 + y * 4 + x, core * 16 + to_y * 4 + to_x))
    return lax.ppermute(value, ("core", "y", "x"), pairs)


def gather4(own, phase):
    return [own] + [shift_plane(own, phase, -k) for k in (1, 2, 3)]


def scatter4(blocks, phase):
    got = [shift_plane(blocks[k], phase, k).astype(F32) for k in (1, 2, 3)]
    return blocks[0].astype(F32) + (got[0] + got[1] + got[2])


def split4(value):
    rows = value.shape[0] // 4
    return [value[k * rows : (k + 1) * rows] for k in range(4)]


def scatter_ring(value, z, way, ties=()):
    rows = value.shape[0] // 8
    ties = dict(ties)

    def cut(step):
        at = lax.rem(z + 16 + way * step, 8) * rows
        return lax.dynamic_slice_in_dim(value, at, rows, 0)

    steps = (4, 3, -3, 2, -2, 1, -1, 0)
    block = dict(zip(steps, barrier(tuple(cut(step) for step in steps)))).__getitem__

    one, other = shift_z(block(4), 1), None
    for step in (3, 2, 1):
        if step in ties:
            if other is None:
                one, ties[step] = barrier((one, ties[step]))
            else:
                one, other, ties[step] = barrier((one, other, ties[step]))
        one = shift_z(add(block(step), one), 1)
        other = shift_z(block(-step) if other is None else add(block(-step), other), -1)
    return (block(0), one, other), ties


def total3(pieces):
    own, one, other = (piece.astype(F32) for piece in pieces)
    return own + (one + other)


def gather_ring(own, z, way):
    rows = own.shape[0]
    out = jnp.zeros((8 * rows, own.shape[1]), own.dtype)

    def put(out, value, step):
        at = lax.rem(z + 16 + way * step, 8) * rows
        return lax.dynamic_update_slice_in_dim(out, value, at, 0)

    out = put(out, own, 0)
    one = other = own
    for step in (1, 2, 3):
        one, other = shift_z(one, 1), shift_z(other, -1)
        out = put(put(out, one, -step), other, step)
    return put(out, shift_z(one, 1), 4)


def shards(inputs, w_in, w_out, grad_outputs):
    zl = lax.axis_index("zl")
    core = lax.axis_index("core")
    z = lax.axis_index("zh") * 2 + zl
    way = 1 - 2 * core
    rows = inputs.shape[0]
    half = inputs.shape[1] // 2
    quarter = half // 2
    low = zl == 0
    w_in = lax.dynamic_slice_in_dim(w_in, zl * half, half, 0)
    w_out = lax.dynamic_slice_in_dim(w_out, zl * half, half, 1)

    with jax.named_scope("width_swap"):
        pick = lambda here: jnp.concatenate(
            [jnp.where(here, v[:, :half], v[:, half:]) for v in (inputs, grad_outputs)]
        )
        kept = pick(low)
        got = swap(pick(jnp.logical_not(low)), "zl")
        first, second = jnp.where(low, kept, got), jnp.where(low, got, kept)
        own = jnp.concatenate([first[:rows], second[:rows], first[rows:], second[rows:]])
    with jax.named_scope("gather_line"):
        line = gather4(own, 0)
    with jax.named_scope("gather_tokens"):
        tokens = jnp.concatenate(gather4(jnp.concatenate([b[: 2 * rows] for b in line]), 1))
    with jax.named_scope("gather_cots"):
        cots = jnp.concatenate(gather4(jnp.concatenate([b[2 * rows :] for b in line]), 1))

    part = contract(tokens, w_in, 1, 0).astype(BF16)
    grad_part = contract(cots, w_out, 1, 1).astype(BF16)
    with jax.named_scope("scatter_preact"):
        pieces, tied = scatter_ring(part, z, way, {3: grad_part})
    grad_part = tied[3]
    preact = total3(pieces)
    activated = gelu_fn(preact).astype(BF16)
    preact, activated = barrier((preact, activated))
    with jax.named_scope("scatter_grad"):
        pieces, tied = scatter_ring(grad_part, z, way, {1: activated})
    activated = tied[1]
    with jax.named_scope("gather_act"):
        all_act = gather_ring(activated, z, way)
    grad_preact = jax.vjp(gelu_fn, preact)[1](total3(pieces))[0].astype(BF16)
    with jax.named_scope("gather_grad"):
        all_grad = gather_ring(grad_preact, z, way)

    out_part = split4(contract(all_act, w_out, 1, 0).astype(BF16))
    grad_part = contract(all_grad, w_in, 1, 1).astype(BF16)
    with jax.named_scope("scatter_out"):
        out_line = scatter4(out_part, 1).astype(BF16)
    with jax.named_scope("scatter_cot"):
        grad_line = scatter4(split4(grad_part), 1).astype(BF16)
    all_act, _ = barrier((all_act, grad_part))
    all_grad, out_line = barrier((all_grad, out_line))

    def columns(value, at):
        return lax.dynamic_slice_in_dim(value, at * quarter, quarter, 1)

    with jax.named_scope("weight_gradients"):
        sent_out = contract(all_act, columns(cots, 1 - core), 0, 0).astype(BF16)
        sent_in = contract(columns(tokens, 1 - core), all_grad, 0, 0).astype(BF16)
        got_out, got_in = swap(sent_out, "core"), swap(sent_in, "core")
        grad_w_out = (contract(all_act, columns(cots, core), 0, 0) + got_out).astype(BF16)
        grad_w_in = (contract(columns(tokens, core), all_grad, 0, 0) + got_in).astype(BF16)

    lines = [jnp.concatenate([a, b]) for a, b in zip(split4(out_line), split4(grad_line))]
    with jax.named_scope("scatter_line"):
        got = [shift_plane(lines[k], 0, k) for k in (1, 2, 3)]
        got, grad_w_in, grad_w_out = barrier((got, grad_w_in, grad_w_out))
        got = [value.astype(F32) for value in got]
        total = lines[0].astype(F32) + (got[0] + got[1] + got[2])
    with jax.named_scope("token_swap"):
        first = jnp.concatenate([total[:rows], total[2 * rows : 3 * rows]])
        second = jnp.concatenate([total[rows : 2 * rows], total[3 * rows :]])
        kept = jnp.where(low, first, second)
        got = swap(jnp.where(low, second, first).astype(BF16), "zl").astype(F32)
        sums = jnp.concatenate([jnp.where(low, kept, got), jnp.where(low, got, kept)], axis=1)
    outputs = (inputs.astype(F32) + sums[:rows]).astype(BF16)
    grad_inputs = (grad_outputs.astype(F32) + sums[rows:]).astype(BF16)
    return (outputs, grad_inputs, grad_w_in, grad_w_out)


def solution(mesh):
    fine = Mesh(mesh.devices.reshape(2, 2, 4, 4, 4), NAMES)
    activations = P(("zl", "core", "y", "x"), "zh")
    return jax.shard_map(
        shards,
        mesh=fine,
        in_specs=(activations, P("zh", ("y", "x")), P(("y", "x"), "zh"), activations),
        out_specs=(
            activations,
            activations,
            P(("zh", "zl", "core"), ("y", "x")),
            P(("y", "x"), ("zh", "zl", "core")),
        ),
        check_vma=False,
    )
```

```python
import jax
import jax.numpy as jnp
from jax import lax
from jax.sharding import Mesh, PartitionSpec as P

F32 = jnp.float32
BF16 = jnp.bfloat16
NAMES = ("zl", "core", "zh", "y", "x")
barrier = lax.optimization_barrier


def gelu_fn(values):
    return jax.nn.gelu(values, approximate=True)


def contract(left, right, left_dim, right_dim):
    return lax.dot_general(
        left, right, (((left_dim,), (right_dim,)), ((), ())), preferred_element_type=F32
    )


def add(one, other):
    return (one.astype(F32) + other.astype(F32)).astype(BF16)


def swap(value, axis):
    return lax.ppermute(value, axis, [(0, 1), (1, 0)])


def shift_z(value, way):
    place = lambda z, core: (z % 2) * 8 + core * 4 + (z % 8) // 2
    pairs = [
        (place(z, core), place((z + way * (1 - 2 * core)) % 8, core))
        for core in range(2)
        for z in range(8)
    ]
    return lax.ppermute(value, ("zl", "core", "zh"), pairs)


def shift_plane(value, phase, step):
    pairs = []
    for core in range(2):
        for y in range(4):
            for x in range(4):
                along_x = core == phase
                to_y = y if along_x else (y + step) % 4
                to_x = (x + step) % 4 if along_x else x
                pairs.append((core * 16 + y * 4 + x, core * 16 + to_y * 4 + to_x))
    return lax.ppermute(value, ("core", "y", "x"), pairs)


def gather4(own, phase):
    return [own] + [shift_plane(own, phase, -k) for k in (1, 2, 3)]


def scatter4(blocks, phase):
    got = [shift_plane(blocks[k], phase, k).astype(F32) for k in (1, 2, 3)]
    return blocks[0].astype(F32) + (got[0] + got[1] + got[2])


def split4(value):
    rows = value.shape[0] // 4
    return [value[k * rows : (k + 1) * rows] for k in range(4)]


def scatter_ring(value, z, way, ties=()):
    rows = value.shape[0] // 8
    ties = dict(ties)

    def cut(step):
        at = lax.rem(z + 16 + way * step, 8) * rows
        return lax.dynamic_slice_in_dim(value, at, rows, 0)

    steps = (4, 3, -3, 2, -2, 1, -1, 0)
    block = dict(zip(steps, barrier(tuple(cut(step) for step in steps)))).__getitem__

    one, other = shift_z(block(4), 1), None
    for step in (3, 2, 1):
        if step in ties:
            if other is None:
                one, ties[step] = barrier((one, ties[step]))
            else:
                one, other, ties[step] = barrier((one, other, ties[step]))
        one = shift_z(add(block(step), one), 1)
        other = shift_z(block(-step) if other is None else add(block(-step), other), -1)
    return (block(0), one, other), ties


def total3(pieces):
    own, one, other = (piece.astype(F32) for piece in pieces)
    return own + (one + other)


def gather_ring(own, z, way):
    rows = own.shape[0]
    out = jnp.zeros((8 * rows, own.shape[1]), own.dtype)

    def put(out, value, step):
        at = lax.rem(z + 16 + way * step, 8) * rows
        return lax.dynamic_update_slice_in_dim(out, value, at, 0)

    out = put(out, own, 0)
    one = other = own
    for step in (1, 2, 3):
        one, other = shift_z(one, 1), shift_z(other, -1)
        out = put(put(out, one, -step), other, step)
    return put(out, shift_z(one, 1), 4)


def shards(inputs, w_in, w_out, grad_outputs):
    zl = lax.axis_index("zl")
    core = lax.axis_index("core")
    z = lax.axis_index("zh") * 2 + zl
    way = 1 - 2 * core
    rows = inputs.shape[0]
    half = inputs.shape[1] // 2
    quarter = half // 2
    low = zl == 0
    w_in = lax.dynamic_slice_in_dim(w_in, zl * half, half, 0)
    w_out = lax.dynamic_slice_in_dim(w_out, zl * half, half, 1)

    with jax.named_scope("width_swap"):
        pick = lambda here: jnp.concatenate(
            [jnp.where(here, v[:, :half], v[:, half:]) for v in (inputs, grad_outputs)]
        )
        kept = pick(low)
        got = swap(pick(jnp.logical_not(low)), "zl")
        first, second = jnp.where(low, kept, got), jnp.where(low, got, kept)
        own = jnp.concatenate([first[:rows], second[:rows], first[rows:], second[rows:]])
    with jax.named_scope("gather_line"):
        line = gather4(own, 0)
    with jax.named_scope("gather_tokens"):
        tokens = jnp.concatenate(gather4(jnp.concatenate([b[: 2 * rows] for b in line]), 1))
    with jax.named_scope("gather_cots"):
        cots = jnp.concatenate(gather4(jnp.concatenate([b[2 * rows :] for b in line]), 1))

    part = contract(tokens, w_in, 1, 0).astype(BF16)
    grad_part = contract(cots, w_out, 1, 1).astype(BF16)
    with jax.named_scope("scatter_preact"):
        pieces, tied = scatter_ring(part, z, way, {3: grad_part})
    grad_part = tied[3]
    preact = total3(pieces)
    activated = gelu_fn(preact).astype(BF16)
    slope = jax.vjp(gelu_fn, preact)[1](jnp.ones_like(preact))[0]
    slope, activated = barrier((slope, activated))
    with jax.named_scope("scatter_grad"):
        pieces, tied = scatter_ring(grad_part, z, way, {1: activated})
    activated = tied[1]
    with jax.named_scope("gather_act"):
        all_act = gather_ring(activated, z, way)
    grad_preact = (slope * total3(pieces)).astype(BF16)
    with jax.named_scope("gather_grad"):
        all_grad = gather_ring(grad_preact, z, way)

    out_part = split4(contract(all_act, w_out, 1, 0).astype(BF16))
    grad_part = contract(all_grad, w_in, 1, 1).astype(BF16)
    with jax.named_scope("scatter_out"):
        out_line = scatter4(out_part, 1).astype(BF16)
    with jax.named_scope("scatter_cot"):
        grad_line = scatter4(split4(grad_part), 1).astype(BF16)
    all_act, _ = barrier((all_act, grad_part))
    all_grad, out_line = barrier((all_grad, out_line))

    def columns(value, at):
        return lax.dynamic_slice_in_dim(value, at * quarter, quarter, 1)

    with jax.named_scope("weight_gradients"):
        sent_out = contract(all_act, columns(cots, 1 - core), 0, 0).astype(BF16)
        sent_in = contract(columns(tokens, 1 - core), all_grad, 0, 0).astype(BF16)
        got_out, got_in = swap(sent_out, "core"), swap(sent_in, "core")
        grad_w_out = (contract(all_act, columns(cots, core), 0, 0) + got_out).astype(BF16)
        grad_w_in = (contract(columns(tokens, core), all_grad, 0, 0) + got_in).astype(BF16)

    lines = [jnp.concatenate([a, b]) for a, b in zip(split4(out_line), split4(grad_line))]
    with jax.named_scope("scatter_line"):
        got = [shift_plane(lines[k], 0, k) for k in (1, 2, 3)]
        got, grad_w_in, grad_w_out = barrier((got, grad_w_in, grad_w_out))
        got = [value.astype(F32) for value in got]
        total = lines[0].astype(F32) + (got[0] + got[1] + got[2])
    with jax.named_scope("token_swap"):
        first = jnp.concatenate([total[:rows], total[2 * rows : 3 * rows]])
        second = jnp.concatenate([total[rows : 2 * rows], total[3 * rows :]])
        kept = jnp.where(low, first, second)
        got = swap(jnp.where(low, second, first).astype(BF16), "zl").astype(F32)
        sums = jnp.concatenate([jnp.where(low, kept, got), jnp.where(low, got, kept)], axis=1)
    outputs = (inputs.astype(F32) + sums[:rows]).astype(BF16)
    grad_inputs = (grad_outputs.astype(F32) + sums[rows:]).astype(BF16)
    return (outputs, grad_inputs, grad_w_in, grad_w_out)


def solution(mesh):
    fine = Mesh(mesh.devices.reshape(2, 2, 4, 4, 4), NAMES)
    activations = P(("zl", "core", "y", "x"), "zh")
    return jax.shard_map(
        shards,
        mesh=fine,
        in_specs=(activations, P("zh", ("y", "x")), P(("y", "x"), "zh"), activations),
        out_specs=(
            activations,
            activations,
            P(("zh", "zl", "core"), ("y", "x")),
            P(("y", "x"), ("zh", "zl", "core")),
        ),
        check_vma=False,
    )
```
